32 devices in a mesh: pool: 2 (over y), grp: 4 (over x, core), shard: 4 (over z).
Axes of the slice: x: 2, y: 2, z: 4, core: 2. Of those that a mesh axis runs over, the one named last changes fastest.
Arguments:
- queries: bfloat16 [128, 6144], P(('pool', 'grp', 'shard')), may hold values from -160 to 160
- new_kv: bfloat16 [128, 2, 1024], P(('pool', 'grp', 'shard')), may hold values from -8 to 8
- suffix_kv: bfloat16 [128, 64, 2, 1024], P(('pool', 'grp', 'shard')), may hold values from -8 to 8
- suffix_len: int32 [128], P(('pool', 'grp', 'shard')), may hold values from 1 to 64, 4096 in all
- prefix_pool: bfloat16 [32, 6, 128, 2, 1024], P(('pool', 'grp', 'shard')), may hold values from -6 to 6
- prefix_table: int32 [32, 4], P(('pool', 'grp', 'shard')), may hold values from 0 to 5, as said below
- residual: bfloat16 [128, 6144], P(('pool', 'grp', 'shard')), may hold values from -6 to 6
- norm_gain: bfloat16 [6144], replicated, may hold values from 0.099609375 to 1.8984375
- expert_ids: int32 [128, 2], P(('pool', 'grp', 'shard')), may hold values from 0 to 7, as said below
- gate_weights: float32 [128, 2], P(('pool', 'grp', 'shard')), may hold values from 0.1 to 1
- expert_in: bfloat16 [8, 6144, 2, 8192], P('grp', None, None, ('pool', 'shard')), may hold values from -0.078125 to 0.078125
- expert_down: bfloat16 [8, 8192, 6144], P('grp', ('pool', 'shard')), may hold values from -0.0625 to 0.0625
Outputs:
- attended: bfloat16 [128, 6144], P(('pool', 'grp', 'shard'))
- layer_out: bfloat16 [128, 6144], P(('pool', 'grp', 'shard'))
The draws below stay inside these ranges and needn't reach their ends.
Inputs may be any that keep to these rules, and one draw needn't show every extreme that they name: `prefix_table`: each device's 4 entries are different blocks of its pool. `expert_ids`: each row names two different experts. One expert, the same for all devices, is named by exactly 2 of the 4 rows of every device; no expert is named by more than 2 rows of one device.
All inputs are finite; a program needn't handle non-finite values. No bound on the sum of `suffix_len` on one device may be relied on, other than what follows from the above.
Results may differ from the reference program's by a relative error of at most 0.013.
Values may be sent and summed in bfloat16 or wider, within the bound.
No kernel may reach another device: no remote copies, remote signals or barrier semaphores. Data moves between devices by JAX's collectives and lax.ppermute only.
A program may use at most 192 MiB of HBM per device.

```python
import math
import jax
import jax.numpy as jnp
import numpy as np
from jax import lax

D = 6144
QH = 48
KVH = 8
HD = 128
EXPERTS = 8
FF = 8192
BLK = 128
REQ_DEV = 4
SUF = 64
PB = 4
CAP = 2
NPOOL = 6
REQUESTS = 128
DEVICES = 32


def suffix_key_base(key):
    return jax.random.normal(jax.random.fold_in(key, 77), (REQUESTS, SUF, KVH * HD), jnp.float32)


def draw_suffix_kv(key, part):
    shared = suffix_key_base(key)
    key = jax.random.fold_in(key, 1)
    values = jax.random.normal(key, (REQUESTS, SUF, KVH * HD), jnp.float32)
    return jnp.stack([shared, values], axis=2).astype(jnp.bfloat16)


def draw_queries(key, part):
    key = jax.random.fold_in(key, 2)
    groups = QH // KVH
    result = 2.0 * jax.random.normal(key, (REQUESTS, KVH, groups, HD), jnp.float32)
    return result.reshape(REQUESTS, QH * HD).astype(jnp.bfloat16)


def draw_new_kv(key, part):
    key = jax.random.fold_in(key, 3)
    key_keys, key_values = jax.random.split(key)
    fresh_keys = jax.random.normal(key_keys, (REQUESTS, KVH * HD), jnp.float32)
    fresh_values = jax.random.normal(key_values, (REQUESTS, KVH * HD), jnp.float32)
    return jnp.stack([fresh_keys, fresh_values], axis=1).astype(jnp.bfloat16)


def draw_prefix_table(key, part):
    key = jax.random.fold_in(key, 4)
    device_keys = jax.random.split(key, DEVICES)
    return jax.vmap(lambda dev_key: jax.random.permutation(dev_key, NPOOL)[:PB])(device_keys).astype(jnp.int32)


def draw_expert_ids(key, part):
    key = jax.random.fold_in(key, 5)
    favored_key, device_key = jax.random.split(key)
    favored = jax.random.randint(favored_key, (), 0, EXPERTS)
    device_keys = jax.random.split(device_key, DEVICES)

    def one_device(dev_key):
        key_rows, key_cycle, key_swap = jax.random.split(dev_key, 3)
        row_order = jax.random.permutation(key_rows, REQ_DEV)
        is_favored = row_order < CAP
        other_cycle = jax.random.permutation(key_cycle, EXPERTS - 1)
        needed = jnp.where(is_favored, 1, 2).astype(jnp.int32)
        start_at = jnp.cumsum(needed) - needed
        first_other = (favored + 1 + other_cycle[start_at % (EXPERTS - 1)]) % EXPERTS
        second_other = (favored + 1 + other_cycle[(start_at + 1) % (EXPERTS - 1)]) % EXPERTS
        swap_bit = jax.random.randint(key_swap, (REQ_DEV,), 0, 2)
        column_a = jnp.where(is_favored, jnp.where(swap_bit == 1, first_other, favored), first_other)
        column_b = jnp.where(is_favored, jnp.where(swap_bit == 1, favored, first_other), second_other)
        return jnp.stack([column_a, column_b], axis=1).astype(jnp.int32)
    return jax.vmap(one_device)(device_keys).reshape(REQUESTS, 2).astype(jnp.int32)


def block_scale(rng, dims, cuts, low, top_value):
    def one(axis_at, parts):
        steps = jax.random.uniform(jax.random.fold_in(jax.random.fold_in(rng, 6), axis_at), (parts,), jnp.float32, low / len(cuts), top_value / len(cuts))
        return jnp.repeat(jnp.exp(steps), dims[axis_at] // parts).reshape((-1,) + (1,) * (len(dims) - axis_at - 1))

    gain = one(*cuts[0])
    for cut in cuts[1:]:
        gain = gain * one(*cut)
    return gain


def split_up(number_of, total, limit, lean):
    loads = [(1 << 20) // math.isqrt(rank ** lean) + 1 for rank in range(2, number_of + 1)]
    rest, given = total - limit - (number_of - 1), [1] * (number_of - 1)
    while rest > 0:
        candidates = [i for i in range(number_of - 1) if given[i] < limit]
        whole, remaining = sum([loads[i] for i in candidates]), rest
        for i in candidates:
            extra = min(limit - given[i], max(1, remaining * loads[i] // whole), rest)
            given[i] = given[i] + extra
            rest = rest - extra
    return np.array([limit] + given)


def uneven_parts(stream_key, count, total, limit, skew):
    if count == 2:
        one = jax.random.randint(stream_key, (), max(1, total - limit), min(limit, total - 1) + 1)
        return jnp.stack([one, total - one])
    lengths = jnp.asarray(split_up(count, total, limit, skew), jnp.int32)
    twos = (count - 1) // 2
    giver, receiver = lengths[1:1 + 2 * twos:2], lengths[2:2 + 2 * twos:2]
    margin = jnp.minimum(giver - 1, limit - receiver)
    passed = jax.random.randint(jax.random.fold_in(stream_key, 1), (twos,), 0, 1 << 20) % (margin + 1)
    lengths = lengths.at[1:1 + 2 * twos:2].set(giver - passed).at[2:2 + 2 * twos:2].set(receiver + passed)
    return lengths[jax.random.permutation(jax.random.fold_in(stream_key, 2), count)]


def centred(own_key, extent, deviation, limit, pieces=(), kind=jnp.bfloat16):
    values = deviation * jax.random.normal(own_key, extent, jnp.float32)
    if pieces:
        values = values * block_scale(own_key, extent, pieces, -0.22, 0.18)
    return jnp.clip(values, -limit, limit).astype(kind)


def setup_inputs(seed: int = 0) -> dict:
    arg_keys = jax.random.split(jax.random.key(seed), 13)
    return {
        "queries": draw_queries(jax.random.fold_in(arg_keys[12], 71), 0),
        "new_kv": draw_new_kv(jax.random.fold_in(arg_keys[12], 71), 0),
        "suffix_kv": draw_suffix_kv(jax.random.fold_in(arg_keys[12], 71), 0),
        "suffix_len": uneven_parts(arg_keys[3], REQUESTS, REQUESTS * SUF // 2, SUF, 2).astype(jnp.int32),
        "prefix_pool": centred(arg_keys[4], (DEVICES, NPOOL, BLK, 2, KVH * HD), 1.0, 6.0, ((0, 32),)),
        "prefix_table": draw_prefix_table(jax.random.fold_in(arg_keys[12], 71), 0),
        "residual": centred(arg_keys[6], (REQUESTS, D), 1.0, 6.0, ((0, 32),)),
        "norm_gain": jnp.clip(1.0 + 0.18 * jax.random.normal(arg_keys[7], (D,), jnp.float32), 0.099609375, 1.8984375).astype(jnp.bfloat16),
        "expert_ids": draw_expert_ids(jax.random.fold_in(arg_keys[12], 71), 0),
        "gate_weights": jnp.clip(0.1 + 0.9 * jax.random.uniform(arg_keys[9], (REQUESTS, 2), jnp.float32) ** block_scale(arg_keys[9], (REQUESTS, 2), ((0, 32),), -0.2, 0.2), 0.1, 1.0),
        "expert_in": centred(arg_keys[10], (EXPERTS, D, 2, FF), D ** -0.5, 0.078125, ((0, 4), (3, 8))),
        "expert_down": centred(arg_keys[11], (EXPERTS, FF, D), FF ** -0.5, 0.0625, ((0, 4), (1, 8))),
    }


def attend_device(operands):
    queries, new_kv, suffix_kv, suffix_len, pool_blocks, block_ids = operands
    groups = QH // KVH
    chosen = jnp.take(pool_blocks, block_ids, axis=0).reshape(PB * BLK, 2, KVH, HD).astype(jnp.float32)
    query_heads = queries.reshape(REQ_DEV, KVH, groups, HD).astype(jnp.float32)
    suffix = suffix_kv.reshape(REQ_DEV, SUF, 2, KVH, HD).astype(jnp.float32)
    fresh = new_kv.reshape(REQ_DEV, 2, KVH, HD).astype(jnp.float32)
    factor = 1.0 / math.sqrt(HD)
    score_pre = jnp.einsum('rkgd,tkd->rkgt', query_heads, chosen[:, 0]) * factor
    score_suf = jnp.einsum('rkgd,rjkd->rkgj', query_heads, suffix[:, :, 0]) * factor
    valid = (jnp.arange(SUF)[None, :] < suffix_len[:, None])[:, None, None, :]
    score_suf = jnp.where(valid, score_suf, -1e+30)
    score_new = jnp.einsum('rkgd,rkd->rkg', query_heads, fresh[:, 0])[..., None] * factor
    scores = jnp.concatenate([score_pre, score_suf, score_new], axis=-1)
    highest = lax.optimization_barrier(jnp.max(scores, axis=-1, keepdims=True))
    weights = jnp.exp(scores - highest)
    probs = (weights / lax.optimization_barrier(jnp.sum(weights, axis=-1, keepdims=True))).astype(jnp.bfloat16).astype(jnp.float32)
    prefix_len = PB * BLK
    result = jnp.einsum('rkgt,tkd->rkgd', probs[..., :prefix_len], chosen[:, 1])
    result = result + jnp.einsum('rkgj,rjkd->rkgd', probs[..., prefix_len:prefix_len + SUF], suffix[:, :, 1])
    result = result + probs[..., prefix_len + SUF:] * fresh[:, 1][:, :, None, :]
    return result.reshape(REQ_DEV, QH * HD).astype(jnp.bfloat16)

def expert_block(operands):
    block_rows, weight_in, weight_down = operands
    hidden_pre = jnp.dot(block_rows, weight_in.reshape(D, 2 * FF), preferred_element_type=jnp.float32)
    hidden_pre = hidden_pre.reshape(-1, 2, FF)
    hidden = (jax.nn.silu(hidden_pre[:, 0]) * hidden_pre[:, 1]).astype(jnp.bfloat16)
    return jnp.dot(hidden, weight_down, preferred_element_type=jnp.float32)

def reference(queries, new_kv, suffix_kv, suffix_len, prefix_pool, prefix_table, residual, norm_gain, expert_ids, gate_weights, expert_in, expert_down):
    attended = lax.map(attend_device, (queries.reshape(DEVICES, REQ_DEV, QH * HD), new_kv.reshape(DEVICES, REQ_DEV, 2, KVH * HD), suffix_kv.reshape(DEVICES, REQ_DEV, SUF, 2, KVH * HD), suffix_len.reshape(DEVICES, REQ_DEV), prefix_pool, prefix_table)).reshape(REQUESTS, QH * HD)
    stream = (residual.astype(jnp.float32) + attended.astype(jnp.float32)).astype(jnp.bfloat16)
    stream_f = stream.astype(jnp.float32)
    normed = (stream_f * lax.rsqrt(lax.optimization_barrier(jnp.mean(stream_f * stream_f, axis=-1, keepdims=True)) + 1e-05) * norm_gain.astype(jnp.float32)).astype(jnp.bfloat16)
    device_ids = expert_ids.reshape(DEVICES, REQ_DEV * 2)
    one_hot = (device_ids[..., None] == jnp.arange(EXPERTS)[None, None, :]).astype(jnp.int32)
    before = jnp.cumsum(one_hot, axis=1) - one_hot
    rank_own = lax.optimization_barrier(jnp.sum(before * one_hot, axis=-1))
    target = device_ids * (DEVICES * CAP) + jnp.arange(DEVICES, dtype=jnp.int32)[:, None] * CAP + rank_own
    target = target.reshape(-1).astype(jnp.int32)
    repeated = jnp.repeat(normed, 2, axis=0)
    buffer = jnp.zeros((EXPERTS * DEVICES * CAP, D), jnp.bfloat16).at[target].set(repeated)
    results = lax.map(expert_block, (buffer.reshape(EXPERTS, DEVICES * CAP, D), expert_in, expert_down))
    expert_out = results.reshape(EXPERTS * DEVICES * CAP, D)[target].reshape(REQUESTS, 2, D)
    layer_out = stream_f + gate_weights[:, 0:1] * expert_out[:, 0] + gate_weights[:, 1:2] * expert_out[:, 1]
    return (attended, layer_out.astype(jnp.bfloat16))
```

```python
import functools
import math

import jax
import jax.numpy as jnp
from jax import lax
from jax.experimental import pallas as pl
from jax.experimental.pallas import tpu as pltpu
from jax.sharding import PartitionSpec as P

QH = 48
KVH = 8
HD = 128
EXPERTS = 8
BLK = 128
SUF = 64
ALL = ("pool", "grp", "shard")
F32 = jnp.float32
BF16 = jnp.bfloat16
LANES = 128
FIELDS = 5


def attend_kernel(
    table, lens, q_ref, new_ref, suf_ref, pool_ref, res_ref, gain_ref, ids_ref, gate_ref,
    att_ref, sent_ref, kv, att_f, sem,
):
    reqs, width = q_ref.shape
    groups = QH // KVH
    blocks = table.shape[1]
    pool_rows = pool_ref.shape[1] * 2 * BLK
    pre, suf = blocks * 2 * BLK, reqs * SUF * 2
    total = kv.shape[1]
    pool2 = pool_ref.reshape(pool_rows, KVH * HD)
    suf2 = suf_ref.reshape(suf, KVH * HD)

    def copies(k):
        cols = pl.ds(k * HD, HD)
        out = [
            pltpu.make_async_copy(
                pool2.at[pl.ds(table[0, b] * (2 * BLK), 2 * BLK), cols],
                kv.at[k, pl.ds(b * 2 * BLK, 2 * BLK)],
                sem.at[k, b],
            )
            for b in range(blocks)
        ]
        out.append(pltpu.make_async_copy(suf2.at[:, cols], kv.at[k, pl.ds(pre, suf)], sem.at[k, blocks]))
        return out

    for k in range(KVH):
        for c in copies(k):
            c.start()

    fresh = new_ref[...].astype(F32).reshape(2 * reqs, KVH * HD)
    fresh = jnp.concatenate([fresh, jnp.zeros((16 - 2 * reqs, KVH * HD), F32)], axis=0).astype(BF16)
    qf = q_ref[...].astype(F32)
    row = lax.broadcasted_iota(jnp.int32, (groups * reqs, total), 0)
    col = lax.broadcasted_iota(jnp.int32, (groups * reqs, total), 1)
    req = row % reqs
    own_len = jnp.zeros_like(row)
    for r in range(reqs):
        own_len = jnp.where(req == r, lens[r], own_len)
    after = col - pre
    fresh_at = after - suf
    ok_suf = (after >= 0) & (after < suf) & (after // (2 * SUF) == req) & ((after % (2 * SUF)) // 2 < own_len)
    ok_new = (fresh_at >= 0) & (fresh_at // 2 == req)
    valid = (col % 2 == 0) & ((col < pre) | ok_suf | ok_new)
    factor = 1.0 / math.sqrt(HD)

    for k in range(KVH):
        kv[k, pre + suf :, :] = jnp.zeros((total - pre - suf, HD), BF16)
        kv[k, pre + suf : pre + suf + 16, :] = fresh[:, k * HD : (k + 1) * HD]
        for c in copies(k):
            c.wait()
        q = jnp.concatenate(
            [qf[:, (k * groups + g) * HD : (k * groups + g + 1) * HD] for g in range(groups)], axis=0
        ).astype(BF16)
        pairs = kv[k]
        scores = lax.dot_general(q, pairs, (((1,), (1,)), ((), ())), preferred_element_type=F32) * factor
        scores = jnp.where(valid, scores, -1e30)
        highest = jnp.max(scores, axis=1, keepdims=True)
        weights = jnp.where(valid, jnp.exp(scores - highest), 0.0)
        probs = weights / jnp.sum(weights, axis=1, keepdims=True)
        probs = pltpu.roll(probs, 1, 1).astype(BF16)
        got = jnp.dot(probs, pairs, preferred_element_type=F32)
        for g in range(groups):
            h = k * groups + g
            att_f[:, h * HD : (h + 1) * HD] = got[g * reqs : (g + 1) * reqs]

    attended = att_f[...].astype(BF16)
    att_ref[...] = attended
    stream = (res_ref[...].astype(F32) + attended.astype(F32)).astype(BF16).astype(F32)
    mean = jnp.sum(stream * stream, axis=1, keepdims=True) * (1.0 / width)
    normed = stream * lax.rsqrt(mean + 1e-05) * gain_ref[...].astype(F32)
    sent_ref[:, :width] = normed.astype(BF16)

    lane = lax.broadcasted_iota(jnp.int32, (reqs, LANES), 1)
    expert, field = lane % EXPERTS, lane // EXPERTS
    first, second = ids_ref[:, 0:1] == expert, ids_ref[:, 1:2] == expert
    gate = jnp.where(first, gate_ref[:, 0:1], 0.0) + jnp.where(second, gate_ref[:, 1:2], 0.0)
    high = gate.astype(BF16).astype(F32)
    mid = (gate - high).astype(BF16).astype(F32)
    low = gate - high - mid
    member = (first | second).astype(F32)
    before = [jnp.zeros((1, LANES), F32)]
    for r in range(reqs - 1):
        before.append(before[-1] + member[r : r + 1])
    before = jnp.concatenate(before, axis=0)
    record = jnp.where(field == 0, high, jnp.where(field == 1, mid, jnp.where(field == 2, low, 0.0)))
    record = jnp.where((field == 3) & (before == 0.0), member, record)
    record = jnp.where((field == 4) & (before == 1.0), member, record)
    sent_ref[:, width:] = record.astype(BF16)


def attend(queries, new_kv, suffix_kv, suffix_len, pool, table, residual, gain, ids, gates):
    reqs, width = queries.shape
    total = table.shape[1] * 2 * BLK + reqs * SUF * 2 + LANES
    vmem = pl.BlockSpec(memory_space=pltpu.VMEM)
    smem = pl.BlockSpec(memory_space=pltpu.SMEM)
    hbm = pl.BlockSpec(memory_space=pl.ANY)
    return pl.pallas_call(
        attend_kernel,
        out_shape=(
            jax.ShapeDtypeStruct((reqs, width), BF16),
            jax.ShapeDtypeStruct((reqs, width + LANES), BF16),
        ),
        in_specs=[smem, smem, vmem, vmem, hbm, hbm, vmem, vmem, vmem, vmem],
        out_specs=(vmem, vmem),
        scratch_shapes=[
            pltpu.VMEM((KVH, total, HD), BF16),
            pltpu.VMEM((reqs, width), F32),
            pltpu.SemaphoreType.DMA((KVH, table.shape[1] + 1)),
        ],
        compiler_params=pltpu.CompilerParams(vmem_limit_bytes=24 * 2**20),
    )(table, suffix_len, queries, new_kv, suffix_kv, pool, residual, gain.reshape(1, width), ids, gates)


RING = 4
STEP = 768
DOWN = 512


def expert_kernel(parts, reqs, base_ref, *refs):
    x_refs = refs[:parts]
    in_ref, down_ref, near_ref, far_ref, wide, lhs, ring, down, acc, dense, ring_sem, down_sem = refs[parts:]
    experts, depth, _, units = in_ref.shape
    rows = near_ref.shape[0] * 2
    slots = rows // 2
    steps = depth // STEP
    tiles = units // LANES
    cuts = depth // DOWN
    in2 = in_ref.reshape(experts, 2 * depth, units)

    def in_copies(i):
        e, s = divmod(i, steps)
        return [
            pltpu.make_async_copy(
                in2.at[e, pl.ds(s * 2 * STEP, 2 * STEP), pl.ds(j * LANES, LANES)],
                ring.at[i % RING, j],
                ring_sem.at[i % RING, j],
            )
            for j in range(tiles)
        ]

    def down_copy(c):
        return pltpu.make_async_copy(
            down_ref.at[:, :, pl.ds(c * DOWN, DOWN)], down.at[c], down_sem.at[c]
        )

    for i in range(RING):
        for c in in_copies(i):
            c.start()

    part_rows = rows // parts
    for p in range(parts):
        wide[p * part_rows : (p + 1) * part_rows, :] = x_refs[p][...]

    base = base_ref[0]
    record = wide[:, depth:].astype(F32)
    lane = lax.broadcasted_iota(jnp.int32, record.shape, 1)
    row = lax.broadcasted_iota(jnp.int32, (rows, slots), 0)
    slot = lax.broadcasted_iota(jnp.int32, (rows, slots), 1)

    def column(field, e):
        return jnp.sum(jnp.where(lane == field * EXPERTS + e, record, 0.0), axis=1, keepdims=True)

    spread, gates = [], []
    for e in range(experts):
        first, second = column(3, base + e), column(4, base + e)
        gates.append(column(0, base + e) + column(1, base + e) + column(2, base + e))
        spread.append(
            jnp.where(row // reqs == slot // 2, jnp.where(slot % 2 == 0, first, second), 0.0)
        )
    pick = jnp.concatenate(spread, axis=1).T.astype(BF16)
    spread = [s.astype(BF16) for s in spread]
    src = lax.broadcasted_iota(jnp.int32, (LANES, 4 * LANES), 0)
    dst = lax.broadcasted_iota(jnp.int32, (LANES, 4 * LANES), 1)
    weave = (dst % (2 * LANES) == 2 * src + dst // (2 * LANES)).astype(F32).astype(BF16)

    blocks = STEP // LANES
    for s in range(steps):
        x = wide[:, s * STEP : (s + 1) * STEP]
        packed = jnp.dot(pick, x, preferred_element_type=F32).astype(BF16)
        tall = jnp.concatenate([packed[:, b * LANES : (b + 1) * LANES] for b in range(blocks)], axis=0)
        woven = jnp.dot(tall, weave, preferred_element_type=F32).astype(BF16)
        for b in range(blocks):
            at = (s * blocks + b) * 2 * LANES
            for e in range(experts):
                r0 = (b * experts + e) * slots
                lhs[e, 0:slots, at : at + 2 * LANES] = woven[r0 : r0 + slots, : 2 * LANES]
                lhs[e, slots : 2 * slots, at : at + 2 * LANES] = woven[r0 : r0 + slots, 2 * LANES :]

    for c in range(cuts):
        down_copy(c).start()

    for e in range(experts):
        for s in range(steps):
            i = e * steps + s
            for c in in_copies(i):
                c.wait()
            x = lhs[e, :, s * 2 * STEP : (s + 1) * 2 * STEP]
            for j in range(0, tiles, 2):
                w = jnp.concatenate([ring[i % RING, j], ring[i % RING, j + 1]], axis=1)
                got = jnp.dot(x, w, preferred_element_type=F32)
                cols = slice(j * LANES, (j + 2) * LANES)
                if s == 0:
                    acc[:, cols] = got
                else:
                    acc[:, cols] += got
            if i + RING < experts * steps:
                for c in in_copies(i + RING):
                    c.start()
        gate, up = acc[:slots, :], acc[slots:, :]
        hidden = (gate / (1.0 + jnp.exp(-gate)) * up).astype(BF16)
        dense[e] = jnp.dot(spread[e], hidden, preferred_element_type=F32).astype(BF16)

    for c in range(cuts):
        down_copy(c).wait()
        for j in range(0, DOWN, 2 * LANES):
            out = gates[0] * jnp.dot(dense[0], down[c, 0, :, j : j + 2 * LANES], preferred_element_type=F32)
            for e in range(1, experts):
                out += gates[e] * jnp.dot(
                    dense[e], down[c, e, :, j : j + 2 * LANES], preferred_element_type=F32
                )
            out = out.astype(BF16)
            cols = slice(c * DOWN + j, c * DOWN + j + 2 * LANES)
            near_ref[:, cols] = out[: rows // 2]
            far_ref[:, cols] = out[rows // 2 :]


def experts_of(reqs, base, xs, expert_in, expert_down):
    experts, depth, _, units = expert_in.shape
    parts = len(xs)
    rows = parts * xs[0].shape[0]
    vmem = pl.BlockSpec(memory_space=pltpu.VMEM)
    hbm = pl.BlockSpec(memory_space=pl.ANY)
    half = jax.ShapeDtypeStruct((rows // 2, depth), BF16)
    return pl.pallas_call(
        functools.partial(expert_kernel, parts, reqs),
        out_shape=(half, half),
        in_specs=[pl.BlockSpec(memory_space=pltpu.SMEM)] + [vmem] * parts + [hbm, hbm],
        out_specs=(vmem, vmem),
        scratch_shapes=[
            pltpu.VMEM((rows, depth + LANES), BF16),
            pltpu.VMEM((experts, rows, 2 * depth), BF16),
            pltpu.VMEM((RING, units // LANES, 2 * STEP, LANES), BF16),
            pltpu.VMEM((depth // DOWN, experts, units, DOWN), BF16),
            pltpu.VMEM((rows, units), F32),
            pltpu.VMEM((experts, rows, units), BF16),
            pltpu.SemaphoreType.DMA((RING, units // LANES)),
            pltpu.SemaphoreType.DMA((depth // DOWN,)),
        ],
        compiler_params=pltpu.CompilerParams(vmem_limit_bytes=60 * 2**20),
    )(base, *xs, expert_in, expert_down)


def local(
    n_pool, n_grp, n_shard,
    queries, new_kv, suffix_kv, suffix_len, prefix_pool, prefix_table, residual, norm_gain,
    expert_ids, gate_weights, expert_in, expert_down,
):
    reqs, width = queries.shape
    attended, sent = attend(
        queries, new_kv, suffix_kv, suffix_len, prefix_pool, prefix_table, residual, norm_gain,
        expert_ids, gate_weights,
    )
    n_high = n_grp // 2

    def turn(a, d):
        return lax.ppermute(a, "shard", [(i, (i + d) % n_shard) for i in range(n_shard)])

    def across(a, dp, dg):
        pairs = []
        for p in range(n_pool):
            for g in range(n_grp):
                to = (g // 2 + dg) % n_high * 2 + g % 2
                pairs.append((p * n_grp + g, (p + dp) % n_pool * n_grp + to))
        return lax.ppermute(a, ("pool", "grp"), pairs)

    def twin(a):
        return lax.ppermute(a, "grp", [(g, g ^ 1) for g in range(n_grp)])

    offsets = [(dp, dg) for dp in range(n_pool) for dg in range(n_high)][1:]
    column = jnp.concatenate([sent] + [turn(sent, d) for d in range(1, n_shard)], axis=0)
    planes = [column] + [across(column, dp, dg) for dp, dg in offsets]
    planes = planes + [twin(a) for a in planes]

    base = (lax.axis_index("grp") * expert_in.shape[0]).astype(jnp.int32).reshape(1)
    near, far = experts_of(reqs, base, planes, expert_in, expert_down)

    back = twin(far)
    pair = (near.astype(F32) + back.astype(F32)).astype(BF16)
    pair = pair.reshape(1 + len(offsets), reqs * n_shard, width)
    total = pair[0].astype(F32)
    for i, (dp, dg) in enumerate(offsets):
        total += across(pair[i + 1], -dp, -dg).astype(F32)
    total = total.astype(BF16).reshape(n_shard, reqs, width)
    stream = (residual.astype(F32) + attended.astype(F32)).astype(BF16).astype(F32)
    out = stream + total[0].astype(F32)
    for d in range(1, n_shard):
        out += turn(total[d], -d).astype(F32)
    return attended, out.astype(BF16)


def solution(mesh):
    rows = P(ALL, None)
    in_specs = (
        rows,
        P(ALL, None, None),
        P(ALL, None, None, None),
        P(ALL),
        P(ALL, None, None, None, None),
        rows,
        rows,
        P(),
        rows,
        rows,
        P("grp", None, None, ("pool", "shard")),
        P("grp", ("pool", "shard"), None),
    )
    sizes = [mesh.shape[a] for a in ALL]
    return jax.shard_map(
        functools.partial(local, *sizes),
        mesh=mesh, in_specs=in_specs, out_specs=(rows, rows), check_vma=False,
    )
```

```python
import functools
import math

import jax
import jax.numpy as jnp
from jax import lax
from jax.experimental import pallas as pl
from jax.experimental.pallas import tpu as pltpu
from jax.sharding import PartitionSpec as P

QH = 48
KVH = 8
HD = 128
EXPERTS = 8
BLK = 128
SUF = 64
ALL = ("pool", "grp", "shard")
F32 = jnp.float32
BF16 = jnp.bfloat16
LANES = 128
PARTS = 2
STEP = 768
RING = 4


def three_terms(x):
    high = x.astype(BF16).astype(F32)
    mid = (x - high).astype(BF16).astype(F32)
    return high, mid, x - high - mid


def block_copies(in_hbm, part, i, dst, sem):
    experts, depth, _, units = in_hbm.shape
    e, s = divmod(i, depth // PARTS // STEP)
    start = 2 * (part * (depth // PARTS) + s * STEP)
    pairs = in_hbm.reshape(experts, 2 * depth, units)
    return [
        pltpu.make_async_copy(
            pairs.at[e, pl.ds(start, 2 * STEP), pl.ds(j * LANES, LANES)], dst.at[j], sem.at[j]
        )
        for j in range(units // LANES)
    ]


def attend_kernel(
    table_hbm, lens_hbm, ids_hbm, gates_hbm, q_hbm, new_hbm, suf_ref, pool_ref, res_hbm, gain_hbm,
    att_ref, sent_ref,
    kv, att_f, q_ref, new_ref, res_ref, gain_ref, table, lens, ids, gates, sem, small,
):
    reqs, width = q_ref.shape
    groups = QH // KVH
    heads = KVH
    blocks = table.shape[1]
    pool_rows = pool_ref.shape[1] * 2 * BLK
    pre, suf = blocks * 2 * BLK, reqs * SUF * 2
    total = kv.shape[1]
    pool2 = pool_ref.reshape(pool_rows, KVH * HD)
    suf2 = suf_ref.reshape(suf, KVH * HD)

    pairs = [
        (table_hbm, table),
        (q_hbm, q_ref),
        (new_hbm, new_ref),
        (res_hbm, res_ref),
        (gain_hbm, gain_ref),
        (lens_hbm, lens),
        (ids_hbm, ids),
        (gates_hbm, gates),
    ]
    small_copies = [pltpu.make_async_copy(src, dst, small.at[i]) for i, (src, dst) in enumerate(pairs)]
    for c in small_copies:
        c.start()
    copies = []
    for k in range(heads):
        cols = pl.ds(k * HD, HD)
        copies.append(
            pltpu.make_async_copy(suf2.at[:, cols], kv.at[k, pl.ds(pre, suf)], sem.at[k, blocks])
        )
    for c in copies:
        c.start()
    small_copies[0].wait()
    for k in range(heads):
        cols = pl.ds(k * HD, HD)
        for b in range(blocks):
            copies.append(pltpu.make_async_copy(
                pool2.at[pl.ds(table[0, b] * (2 * BLK), 2 * BLK), cols],
                kv.at[k, pl.ds(b * 2 * BLK, 2 * BLK)],
                sem.at[k, b],
            ))
            copies[-1].start()
    for c in small_copies[1:]:
        c.wait()

    row = lax.broadcasted_iota(jnp.int32, (groups * reqs, total), 0)
    col = lax.broadcasted_iota(jnp.int32, (groups * reqs, total), 1)
    req = row % reqs
    own_len = jnp.zeros_like(row)
    for r in range(reqs):
        own_len = jnp.where(req == r, lens[r], own_len)
    after = col - pre
    fresh_at = after - suf
    ok_suf = (after >= 0) & (after < suf) & (after // (2 * SUF) == req) & ((after % (2 * SUF)) // 2 < own_len)
    ok_new = (fresh_at >= 0) & (fresh_at // 2 == req)
    valid = (col % 2 == 0) & ((col < pre) | ok_suf | ok_new)
    factor = 1.0 / math.sqrt(HD)
    for k in range(heads):
        kv[k, pre + suf :, :] = jnp.zeros((total - pre - suf, HD), BF16)

    for c in copies:
        c.wait()
    fresh = new_ref[...].astype(F32).reshape(2 * reqs, KVH * HD)
    fresh = jnp.concatenate([fresh, jnp.zeros((16 - 2 * reqs, KVH * HD), F32)], axis=0).astype(BF16)
    qf = q_ref[...].astype(F32)
    scores = []
    for k in range(heads):
        at = k * HD
        kv[k, pre + suf : pre + suf + 16, :] = fresh[:, at : at + HD]
        q = jnp.concatenate(
            [qf[:, (k * groups + g) * HD : (k * groups + g + 1) * HD] for g in range(groups)], axis=0
        ).astype(BF16)
        one = lax.dot_general(q, kv[k], (((1,), (1,)), ((), ())), preferred_element_type=F32) * factor
        scores.append(jnp.where(valid, one, -1e30))
    scores = jnp.concatenate(scores, axis=0)
    weights = jnp.exp(scores - jnp.max(scores, axis=1, keepdims=True))
    probs = weights * (1.0 / jnp.sum(weights, axis=1, keepdims=True))
    probs = pltpu.roll(probs, 1, 1).astype(BF16)
    for k in range(heads):
        rows = groups * reqs
        got = jnp.dot(probs[k * rows : (k + 1) * rows], kv[k], preferred_element_type=F32)
        for g in range(groups):
            h = k * groups + g
            att_f[:, h * HD : (h + 1) * HD] = got[g * reqs : (g + 1) * reqs]

    attended = att_f[...].astype(BF16)
    att_ref[...] = attended
    stream = (res_ref[...].astype(F32) + attended.astype(F32)).astype(BF16).astype(F32)
    mean = jnp.sum(stream * stream, axis=1, keepdims=True) * (1.0 / width)
    normed = stream * lax.rsqrt(mean + 1e-05) * gain_ref[...].astype(F32).reshape(1, width)
    normed = normed.astype(BF16)
    run = width // PARTS

    lane = lax.broadcasted_iota(jnp.int32, (reqs, LANES), 1)
    expert, field = lane % EXPERTS, lane // EXPERTS
    at = lax.broadcasted_iota(jnp.int32, (reqs, LANES), 0)
    gate = jnp.zeros((reqs, LANES), F32)
    member = jnp.zeros((reqs, LANES), F32)
    for r in range(reqs):
        for i in range(2):
            named = (at == r) & (expert == ids[i, r])
            gate = jnp.where(named, gates[i, r], gate)
            member = jnp.where(named, 1.0, member)
    before = [jnp.zeros((1, LANES), F32)]
    for r in range(reqs - 1):
        before.append(before[-1] + member[r : r + 1])
    before = jnp.concatenate(before, axis=0)
    high, mid, low = three_terms(gate)
    record = jnp.where((field == 3) & (before == 0.0), member, 0.0)
    record = jnp.where((field == 4) & (before == 1.0), member, record)
    record = jnp.where(field == 0, high, jnp.where(field == 1, mid, jnp.where(field == 2, low, record)))
    sent_ref[:, :run] = normed[:, :run]
    sent_ref[:, run : run + LANES] = record.astype(BF16)
    sent_ref[:, run + LANES :] = normed[:, run:]


def attend(table, lens, ids, gates, queries, new_kv, suffix_kv, pool, residual, gain):
    reqs, width = queries.shape
    total = table.shape[1] * 2 * BLK + reqs * SUF * 2 + LANES
    return pl.pallas_call(
        attend_kernel,
        out_shape=(
            jax.ShapeDtypeStruct((reqs, width), BF16),
            jax.ShapeDtypeStruct((reqs, width + LANES), BF16),
        ),
        in_specs=[HBM] * 10,
        out_specs=(VMEM,) * 2,
        scratch_shapes=[
            pltpu.VMEM((KVH, total, HD), BF16),
            pltpu.VMEM((reqs, width), F32),
            pltpu.VMEM((reqs, width), BF16),
            pltpu.VMEM(new_kv.shape, BF16),
            pltpu.VMEM((reqs, width), BF16),
            pltpu.VMEM((width,), BF16),
            pltpu.SMEM(table.shape, jnp.int32),
            pltpu.SMEM(lens.shape, jnp.int32),
            pltpu.SMEM(ids.shape, jnp.int32),
            pltpu.SMEM(gates.shape, F32),
            pltpu.SemaphoreType.DMA((KVH, table.shape[1] + 1)),
            pltpu.SemaphoreType.DMA((8,)),
        ],
        compiler_params=pltpu.CompilerParams(vmem_limit_bytes=10 * 2**20),
        cost_estimate=pl.CostEstimate(flops=10**8, bytes_accessed=20 * 10**6, transcendentals=0),
    )(table, lens, ids, gates, queries, new_kv, suffix_kv, pool, residual, gain)


def field_sum(record, fields, e):
    lane = lax.broadcasted_iota(jnp.int32, record.shape, 1)
    hit = lane == fields[0] * EXPERTS + e
    for f in fields[1:]:
        hit = hit | (lane == f * EXPERTS + e)
    return jnp.sum(jnp.where(hit, record, 0.0), axis=1, keepdims=True)


def spreads(record, base, experts, reqs):
    rows = record.shape[0]
    slots = rows // reqs * 2
    row = lax.broadcasted_iota(jnp.int32, (rows, slots), 0)
    slot = lax.broadcasted_iota(jnp.int32, (rows, slots), 1)
    out = []
    for e in range(experts):
        first, second = field_sum(record, (3,), base + e), field_sum(record, (4,), base + e)
        both = jnp.where(slot % 2 == 0, first, second)
        out.append(jnp.where(row // reqs == slot // 2, both, 0.0))
    return out


def expert_kernel(part, n_parts, reqs, base_ref, *refs):
    x_refs = refs[:n_parts]
    last = part == PARTS - 1
    if last:
        (acc_0, record_0, down, in_hbm, near_ref, far_ref,
         wide, lhs, ring, acc_ref, dense, ring_sem) = refs[n_parts:]
    else:
        in_hbm, acc_ref, record_ref, wide, lhs, ring, ring_sem = refs[n_parts:]
    experts, depth, _, units = in_hbm.shape
    rows = wide.shape[0]
    slots = rows // reqs * 2
    width = depth // PARTS
    steps = width // STEP
    tiles = units // LANES
    from_in = {
        i: block_copies(in_hbm, part, i, ring.at[i % RING], ring_sem.at[i % RING])
        for i in range(experts * steps)
    }
    for i in range(RING):
        for c in from_in[i]:
            c.start()

    part_rows = rows // n_parts
    for p in range(n_parts):
        wide[p * part_rows : (p + 1) * part_rows, :] = x_refs[p][...]

    base = base_ref[0]
    if last:
        record = record_0[...]
    else:
        record = wide[:, width:].astype(F32)
        record_ref[...] = record
    spread = spreads(record, base, experts, reqs)
    pick = jnp.concatenate(spread, axis=1).T.astype(BF16)
    src = lax.broadcasted_iota(jnp.int32, (LANES, 4 * LANES), 0)
    dst = lax.broadcasted_iota(jnp.int32, (LANES, 4 * LANES), 1)
    weave = (dst % (2 * LANES) == 2 * src + dst // (2 * LANES)).astype(F32).astype(BF16)

    blocks = STEP // LANES
    for s in range(steps):
        x = wide[:, s * STEP : (s + 1) * STEP]
        packed = jnp.dot(pick, x, preferred_element_type=F32).astype(BF16)
        tall = jnp.concatenate([packed[:, b * LANES : (b + 1) * LANES] for b in range(blocks)], axis=0)
        woven = jnp.dot(tall, weave, preferred_element_type=F32).astype(BF16)
        for b in range(blocks):
            at = (s * blocks + b) * 2 * LANES
            for e in range(experts):
                r0 = (b * experts + e) * slots
                lhs[e, 0:slots, at : at + 2 * LANES] = woven[r0 : r0 + slots, : 2 * LANES]
                lhs[e, slots : 2 * slots, at : at + 2 * LANES] = woven[r0 : r0 + slots, 2 * LANES :]

    for e in range(experts):
        for s in range(steps):
            i = e * steps + s
            for c in from_in[i]:
                c.wait()
            block = ring.at[i % RING]
            x = lhs[e, :, s * 2 * STEP : (s + 1) * 2 * STEP]
            for j in range(0, tiles, 2):
                w = jnp.concatenate([block[j], block[j + 1]], axis=1)
                got = jnp.dot(x, w, preferred_element_type=F32)
                cols = slice(j * LANES, (j + 2) * LANES)
                if s > 0:
                    acc_ref[e, :, cols] += got
                elif last:
                    acc_ref[e, :, cols] = acc_0[e, :, cols] + got
                else:
                    acc_ref[e, :, cols] = got
            if i + RING < experts * steps:
                for c in from_in[i + RING]:
                    c.start()
    if last:
        gates = []
        for e in range(experts):
            gate, up = acc_ref[e, :slots, :], acc_ref[e, slots:, :]
            hidden = (gate / (1.0 + jnp.exp(-gate)) * up).astype(BF16)
            dense[e] = jnp.dot(spread[e].astype(BF16), hidden, preferred_element_type=F32).astype(BF16)
            gates.append(field_sum(record, (0, 1, 2), base + e))
        for j in range(0, depth, 2 * LANES):
            cols = slice(j, j + 2 * LANES)
            out = gates[0] * jnp.dot(dense[0], down[0, :, cols], preferred_element_type=F32)
            for e in range(1, experts):
                out += gates[e] * jnp.dot(dense[e], down[e, :, cols], preferred_element_type=F32)
            out = out.astype(BF16)
            near_ref[:, cols] = out[: rows // 2]
            far_ref[:, cols] = out[rows // 2 :]


VMEM = pl.BlockSpec(memory_space=pltpu.VMEM)
SMEM = pl.BlockSpec(memory_space=pltpu.SMEM)
HBM = pl.BlockSpec(memory_space=pltpu.HBM)


def experts_of(part, reqs, base, xs, carried, expert_in):
    experts, depth, _, units = expert_in.shape
    n_parts = len(xs)
    rows = n_parts * xs[0].shape[0]
    slots = rows // reqs * 2
    width = depth // PARTS
    last = part == PARTS - 1
    half = jax.ShapeDtypeStruct((rows // 2, depth), BF16)
    acc = (experts, 2 * slots, units)
    blocks = experts * (width // STEP)
    record = jax.ShapeDtypeStruct((rows, LANES), F32)
    scratch = [
        pltpu.VMEM((rows, xs[0].shape[1]), BF16),
        pltpu.VMEM((experts, 2 * slots, 2 * width), BF16),
        pltpu.VMEM((RING, units // LANES, 2 * STEP, LANES), BF16),
    ]
    if last:
        out_shape = (half, half)
        operands = (base, *xs, *carried, expert_in)
        in_specs = [SMEM] + [VMEM] * (n_parts + 3) + [HBM]
        scratch += [
            pltpu.VMEM(acc, F32),
            pltpu.VMEM((experts, rows, units), BF16),
        ]
    else:
        out_shape = (jax.ShapeDtypeStruct(acc, F32), record)
        operands = (base, *xs, expert_in)
        in_specs = [SMEM] + [VMEM] * n_parts + [HBM]
    scratch.append(pltpu.SemaphoreType.DMA((RING, units // LANES)))
    return pl.pallas_call(
        functools.partial(expert_kernel, part, n_parts, reqs),
        out_shape=out_shape,
        in_specs=in_specs,
        out_specs=(VMEM,) * len(out_shape),
        scratch_shapes=scratch,
        compiler_params=pltpu.CompilerParams(vmem_limit_bytes=(22 if last else 21) * 2**20),
        cost_estimate=pl.CostEstimate(flops=10**9, bytes_accessed=100 * 10**6, transcendentals=0),
    )(*operands)


def local(
    n_pool, n_grp, n_shard,
    queries, new_kv, suffix_kv, suffix_len, prefix_pool, prefix_table, residual, norm_gain,
    expert_ids, gate_weights, expert_in, expert_down,
):
    reqs, width = queries.shape
    n_high = n_grp // 2
    flips = n_shard & (n_shard - 1) == 0

    def turn(a, d):
        pairs = [(i, i ^ abs(d) if flips else (i + d) % n_shard) for i in range(n_shard)]
        return lax.ppermute(a, "shard", pairs)

    def across(a, dp, dg):
        pairs = []
        for p in range(n_pool):
            for g in range(n_grp):
                to = (g // 2 + dg) % n_high * 2 + g % 2
                pairs.append((p * n_grp + g, (p + dp) % n_pool * n_grp + to))
        return lax.ppermute(a, ("pool", "grp"), pairs)

    def twin(a):
        return lax.ppermute(a, "grp", [(g, g ^ 1) for g in range(n_grp)])

    offsets = [(dp, dg) for dp in range(n_pool) for dg in range(n_high)][1:]
    base = (lax.axis_index("grp") * expert_in.shape[0]).astype(jnp.int32).reshape(1)

    def in_vmem(array):
        return pltpu.with_memory_space_constraint(array, pltpu.VMEM)

    def in_hbm(*arrays):
        return tuple(pltpu.with_memory_space_constraint(a, pltpu.HBM) for a in arrays)

    attended, sent = attend(
        *in_hbm(
            prefix_table, suffix_len, expert_ids.T, gate_weights.T, queries, new_kv, suffix_kv,
            prefix_pool, residual, norm_gain,
        )
    )
    (expert_in,) = in_hbm(expert_in)
    column = [sent] + [turn(sent, d) for d in range(1, n_shard)]
    cut = width // PARTS + LANES
    columns = [jnp.concatenate(c, axis=0) for c in ([a[:, :cut] for a in column], [a[:, cut:] for a in column])]
    def aside(a):
        return [a] + [across(a, dp, dg) for dp, dg in offsets]

    rows_0 = aside(columns[0])
    rows_0 += [twin(a) for a in rows_0]
    acc, record = experts_of(0, reqs, base, rows_0, (), expert_in)
    rows_1 = aside(columns[1])
    acc, *rows_1 = lax.optimization_barrier((acc, *rows_1))
    rows_1 += [twin(a) for a in rows_1]
    near, far = experts_of(1, reqs, base, rows_1, (acc, record, in_vmem(expert_down)), expert_in)
    pair = (near.astype(F32) + twin(far).astype(F32)).astype(BF16)

    def home_along(a, total):
        a = a.reshape(n_shard, -1, a.shape[1])
        total = total + a[0].astype(F32)
        for d in range(1, n_shard):
            total += turn(a[d], -d).astype(F32)
        return total

    def home_aside(a, total):
        a = a.reshape(1 + len(offsets), -1, a.shape[1])
        total = total + a[0].astype(F32)
        for i, (dp, dg) in enumerate(offsets):
            total += across(a[i + 1], -dp, -dg).astype(F32)
        return total

    stream = (residual.astype(F32) + attended.astype(F32)).astype(BF16).astype(F32)
    out = home_along(home_aside(pair, 0.0).astype(BF16), stream)
    return attended, out.astype(BF16)


def solution(mesh):
    rows = P(ALL, None)
    in_specs = (
        rows,
        P(ALL, None, None),
        P(ALL, None, None, None),
        P(ALL),
        P(ALL, None, None, None, None),
        rows,
        rows,
        P(),
        rows,
        rows,
        P("grp", None, None, ("pool", "shard")),
        P("grp", ("pool", "shard"), None),
    )
    sizes = [mesh.shape[a] for a in ALL]
    return jax.shard_map(
        functools.partial(local, *sizes),
        mesh=mesh, in_specs=in_specs, out_specs=(rows, rows), check_vma=False,
    )
```

```python
import functools
import math

import jax
import jax.numpy as jnp
from jax import lax
from jax.experimental import pallas as pl
from jax.experimental.pallas import tpu as pltpu
from jax.sharding import PartitionSpec as P

QH = 48
KVH = 8
HD = 128
EXPERTS = 8
BLK = 128
SUF = 64
ALL = ("pool", "grp", "shard")
F32 = jnp.float32
BF16 = jnp.bfloat16
LANES = 128
PARTS = 2
STEP = 768
RING = 4


def run_of(part, depth):
    first = depth // 8 * 3
    return (first, depth - first) if part else (0, first)


def three_terms(x):
    high = x.astype(BF16).astype(F32)
    mid = (x - high).astype(BF16).astype(F32)
    return high, mid, x - high - mid


def block_copies(in_hbm, part, i, dst, sem):
    experts, depth, _, units = in_hbm.shape
    first, width = run_of(part, depth)
    e, s = divmod(i, width // STEP)
    start = 2 * (first + s * STEP)
    pairs = in_hbm.reshape(experts, 2 * depth, units)
    return [
        pltpu.make_async_copy(
            pairs.at[e, pl.ds(start, 2 * STEP), pl.ds(j * LANES, LANES)], dst.at[j], sem.at[j]
        )
        for j in range(units // LANES)
    ]


def attend_kernel(
    table_hbm, lens_hbm, ids_hbm, gates_hbm, q_hbm, new_hbm, suf_ref, pool_ref, res_hbm, gain_hbm,
    att_ref, sent_ref,
    kv, att_f, q_ref, new_ref, res_ref, gain_ref, table, lens, ids, gates, sem, small,
):
    reqs, width = q_ref.shape
    groups = QH // KVH
    heads = KVH
    blocks = table.shape[1]
    pool_rows = pool_ref.shape[1] * 2 * BLK
    pre, suf = blocks * 2 * BLK, reqs * SUF * 2
    total = kv.shape[1]
    pool2 = pool_ref.reshape(pool_rows, KVH * HD)
    suf2 = suf_ref.reshape(suf, KVH * HD)

    pairs = [
        (table_hbm, table),
        (q_hbm, q_ref),
        (new_hbm, new_ref),
        (res_hbm, res_ref),
        (gain_hbm, gain_ref),
        (lens_hbm, lens),
        (ids_hbm, ids),
        (gates_hbm, gates),
    ]
    small_copies = [pltpu.make_async_copy(src, dst, small.at[i]) for i, (src, dst) in enumerate(pairs)]
    for c in small_copies:
        c.start()
    copies = []
    for k in range(heads):
        cols = pl.ds(k * HD, HD)
        copies.append(
            pltpu.make_async_copy(suf2.at[:, cols], kv.at[k, pl.ds(pre, suf)], sem.at[k, blocks])
        )
    for c in copies:
        c.start()
    small_copies[0].wait()
    for k in range(heads):
        cols = pl.ds(k * HD, HD)
        for b in range(blocks):
            copies.append(pltpu.make_async_copy(
                pool2.at[pl.ds(table[0, b] * (2 * BLK), 2 * BLK), cols],
                kv.at[k, pl.ds(b * 2 * BLK, 2 * BLK)],
                sem.at[k, b],
            ))
            copies[-1].start()
    for c in small_copies[1:]:
        c.wait()

    row = lax.broadcasted_iota(jnp.int32, (groups * reqs, total), 0)
    col = lax.broadcasted_iota(jnp.int32, (groups * reqs, total), 1)
    req = row % reqs
    own_len = jnp.zeros_like(row)
    for r in range(reqs):
        own_len = jnp.where(req == r, lens[r], own_len)
    after = col - pre
    fresh_at = after - suf
    ok_suf = (after >= 0) & (after < suf) & (after // (2 * SUF) == req) & ((after % (2 * SUF)) // 2 < own_len)
    ok_new = (fresh_at >= 0) & (fresh_at // 2 == req)
    valid = (col % 2 == 0) & ((col < pre) | ok_suf | ok_new)
    factor = 1.0 / math.sqrt(HD)
    for k in range(heads):
        kv[k, pre + suf :, :] = jnp.zeros((total - pre - suf, HD), BF16)

    for c in copies:
        c.wait()
    fresh = new_ref[...].astype(F32).reshape(2 * reqs, KVH * HD)
    fresh = jnp.concatenate([fresh, jnp.zeros((16 - 2 * reqs, KVH * HD), F32)], axis=0).astype(BF16)
    qf = q_ref[...].astype(F32)
    scores = []
    for k in range(heads):
        at = k * HD
        kv[k, pre + suf : pre + suf + 16, :] = fresh[:, at : at + HD]
        q = jnp.concatenate(
            [qf[:, (k * groups + g) * HD : (k * groups + g + 1) * HD] for g in range(groups)], axis=0
        ).astype(BF16)
        one = lax.dot_general(q, kv[k], (((1,), (1,)), ((), ())), preferred_element_type=F32) * factor
        scores.append(jnp.where(valid, one, -1e30))
    scores = jnp.concatenate(scores, axis=0)
    weights = jnp.exp(scores - jnp.max(scores, axis=1, keepdims=True))
    probs = weights * (1.0 / jnp.sum(weights, axis=1, keepdims=True))
    probs = pltpu.roll(probs, 1, 1).astype(BF16)
    for k in range(heads):
        rows = groups * reqs
        got = jnp.dot(probs[k * rows : (k + 1) * rows], kv[k], preferred_element_type=F32)
        for g in range(groups):
            h = k * groups + g
            att_f[:, h * HD : (h + 1) * HD] = got[g * reqs : (g + 1) * reqs]

    attended = att_f[...].astype(BF16)
    att_ref[...] = attended
    stream = (res_ref[...].astype(F32) + attended.astype(F32)).astype(BF16).astype(F32)
    mean = jnp.sum(stream * stream, axis=1, keepdims=True) * (1.0 / width)
    normed = stream * lax.rsqrt(mean + 1e-05) * gain_ref[...].astype(F32).reshape(1, width)
    normed = normed.astype(BF16)
    run = run_of(0, width)[1]

    lane = lax.broadcasted_iota(jnp.int32, (reqs, LANES), 1)
    expert, field = lane % EXPERTS, lane // EXPERTS
    at = lax.broadcasted_iota(jnp.int32, (reqs, LANES), 0)
    gate = jnp.zeros((reqs, LANES), F32)
    member = jnp.zeros((reqs, LANES), F32)
    for r in range(reqs):
        for i in range(2):
            named = (at == r) & (expert == ids[i, r])
            gate = jnp.where(named, gates[i, r], gate)
            member = jnp.where(named, 1.0, member)
    before = [jnp.zeros((1, LANES), F32)]
    for r in range(reqs - 1):
        before.append(before[-1] + member[r : r + 1])
    before = jnp.concatenate(before, axis=0)
    high, mid, low = three_terms(gate)
    record = jnp.where((field == 3) & (before == 0.0), member, 0.0)
    record = jnp.where((field == 4) & (before == 1.0), member, record)
    record = jnp.where(field == 0, high, jnp.where(field == 1, mid, jnp.where(field == 2, low, record)))
    sent_ref[:, :run] = normed[:, :run]
    sent_ref[:, run : run + LANES] = record.astype(BF16)
    sent_ref[:, run + LANES :] = normed[:, run:]


def attend(table, lens, ids, gates, queries, new_kv, suffix_kv, pool, residual, gain):
    reqs, width = queries.shape
    total = table.shape[1] * 2 * BLK + reqs * SUF * 2 + LANES
    return pl.pallas_call(
        attend_kernel,
        out_shape=(
            jax.ShapeDtypeStruct((reqs, width), BF16),
            jax.ShapeDtypeStruct((reqs, width + LANES), BF16),
        ),
        in_specs=[HBM] * 10,
        out_specs=(VMEM,) * 2,
        scratch_shapes=[
            pltpu.VMEM((KVH, total, HD), BF16),
            pltpu.VMEM((reqs, width), F32),
            pltpu.VMEM((reqs, width), BF16),
            pltpu.VMEM(new_kv.shape, BF16),
            pltpu.VMEM((reqs, width), BF16),
            pltpu.VMEM((width,), BF16),
            pltpu.SMEM(table.shape, jnp.int32),
            pltpu.SMEM(lens.shape, jnp.int32),
            pltpu.SMEM(ids.shape, jnp.int32),
            pltpu.SMEM(gates.shape, F32),
            pltpu.SemaphoreType.DMA((KVH, table.shape[1] + 1)),
            pltpu.SemaphoreType.DMA((8,)),
        ],
        compiler_params=pltpu.CompilerParams(vmem_limit_bytes=10 * 2**20),
        cost_estimate=pl.CostEstimate(flops=10**8, bytes_accessed=20 * 10**6, transcendentals=0),
    )(table, lens, ids, gates, queries, new_kv, suffix_kv, pool, residual, gain)


def field_sum(record, fields, e):
    lane = lax.broadcasted_iota(jnp.int32, record.shape, 1)
    hit = lane == fields[0] * EXPERTS + e
    for f in fields[1:]:
        hit = hit | (lane == f * EXPERTS + e)
    return jnp.sum(jnp.where(hit, record, 0.0), axis=1, keepdims=True)


def spreads(record, base, experts, reqs):
    rows = record.shape[0]
    slots = rows // reqs * 2
    row = lax.broadcasted_iota(jnp.int32, (rows, slots), 0)
    slot = lax.broadcasted_iota(jnp.int32, (rows, slots), 1)
    out = []
    for e in range(experts):
        first, second = field_sum(record, (3,), base + e), field_sum(record, (4,), base + e)
        both = jnp.where(slot % 2 == 0, first, second)
        out.append(jnp.where(row // reqs == slot // 2, both, 0.0))
    return out


def expert_kernel(part, n_parts, reqs, base_ref, *refs):
    x_refs = refs[:n_parts]
    last = part == PARTS - 1
    if last:
        (acc_0, record_0, down, in_hbm, near_ref, far_ref,
         wide, lhs, ring, acc_ref, dense, ring_sem) = refs[n_parts:]
    else:
        in_hbm, acc_ref, record_ref, wide, lhs, ring, ring_sem = refs[n_parts:]
    experts, depth, _, units = in_hbm.shape
    rows = wide.shape[0]
    slots = rows // reqs * 2
    width = run_of(part, depth)[1]
    steps = width // STEP
    tiles = units // LANES
    from_in = {
        i: block_copies(in_hbm, part, i, ring.at[i % RING], ring_sem.at[i % RING])
        for i in range(experts * steps)
    }
    for i in range(min(RING, experts * steps)):
        for c in from_in[i]:
            c.start()

    part_rows = rows // n_parts
    for p in range(n_parts):
        wide[p * part_rows : (p + 1) * part_rows, :] = x_refs[p][...]

    base = base_ref[0]
    if last:
        record = record_0[...]
    else:
        record = wide[:, width:].astype(F32)
        record_ref[...] = record
    spread = spreads(record, base, experts, reqs)
    pick = jnp.concatenate(spread, axis=1).T.astype(BF16)
    src = lax.broadcasted_iota(jnp.int32, (LANES, 4 * LANES), 0)
    dst = lax.broadcasted_iota(jnp.int32, (LANES, 4 * LANES), 1)
    weave = (dst % (2 * LANES) == 2 * src + dst // (2 * LANES)).astype(F32).astype(BF16)

    blocks = STEP // LANES
    for s in range(steps):
        x = wide[:, s * STEP : (s + 1) * STEP]
        packed = jnp.dot(pick, x, preferred_element_type=F32).astype(BF16)
        tall = jnp.concatenate([packed[:, b * LANES : (b + 1) * LANES] for b in range(blocks)], axis=0)
        woven = jnp.dot(tall, weave, preferred_element_type=F32).astype(BF16)
        for b in range(blocks):
            at = (s * blocks + b) * 2 * LANES
            for e in range(experts):
                r0 = (b * experts + e) * slots
                lhs[e, 0:slots, at : at + 2 * LANES] = woven[r0 : r0 + slots, : 2 * LANES]
                lhs[e, slots : 2 * slots, at : at + 2 * LANES] = woven[r0 : r0 + slots, 2 * LANES :]

    for e in range(experts):
        for s in range(steps):
            i = e * steps + s
            for c in from_in[i]:
                c.wait()
            block = ring.at[i % RING]
            x = lhs[e, :, s * 2 * STEP : (s + 1) * 2 * STEP]
            for j in range(0, tiles, 2):
                w = jnp.concatenate([block[j], block[j + 1]], axis=1)
                got = jnp.dot(x, w, preferred_element_type=F32)
                cols = slice(j * LANES, (j + 2) * LANES)
                if s > 0:
                    acc_ref[e, :, cols] += got
                elif last:
                    acc_ref[e, :, cols] = acc_0[e, :, cols] + got
                else:
                    acc_ref[e, :, cols] = got
            if i + RING < experts * steps:
                for c in from_in[i + RING]:
                    c.start()
    if last:
        gates = []
        for e in range(experts):
            gate, up = acc_ref[e, :slots, :], acc_ref[e, slots:, :]
            hidden = (gate / (1.0 + jnp.exp(-gate)) * up).astype(BF16)
            dense[e] = jnp.dot(spread[e].astype(BF16), hidden, preferred_element_type=F32).astype(BF16)
            gates.append(field_sum(record, (0, 1, 2), base + e))
        for j in range(0, depth, 2 * LANES):
            cols = slice(j, j + 2 * LANES)
            out = gates[0] * jnp.dot(dense[0], down[0, :, cols], preferred_element_type=F32)
            for e in range(1, experts):
                out += gates[e] * jnp.dot(dense[e], down[e, :, cols], preferred_element_type=F32)
            out = out.astype(BF16)
            near_ref[:, cols] = out[: rows // 2]
            far_ref[:, cols] = out[rows // 2 :]


VMEM = pl.BlockSpec(memory_space=pltpu.VMEM)
SMEM = pl.BlockSpec(memory_space=pltpu.SMEM)
HBM = pl.BlockSpec(memory_space=pltpu.HBM)


def experts_of(part, reqs, base, xs, carried, expert_in):
    experts, depth, _, units = expert_in.shape
    n_parts = len(xs)
    rows = n_parts * xs[0].shape[0]
    slots = rows // reqs * 2
    width = run_of(part, depth)[1]
    last = part == PARTS - 1
    half = jax.ShapeDtypeStruct((rows // 2, depth), BF16)
    acc = (experts, 2 * slots, units)
    blocks = experts * (width // STEP)
    record = jax.ShapeDtypeStruct((rows, LANES), F32)
    scratch = [
        pltpu.VMEM((rows, xs[0].shape[1]), BF16),
        pltpu.VMEM((experts, 2 * slots, 2 * width), BF16),
        pltpu.VMEM((RING, units // LANES, 2 * STEP, LANES), BF16),
    ]
    if last:
        out_shape = (half, half)
        operands = (base, *xs, *carried, expert_in)
        in_specs = [SMEM] + [VMEM] * (n_parts + 3) + [HBM]
        scratch += [
            pltpu.VMEM(acc, F32),
            pltpu.VMEM((experts, rows, units), BF16),
        ]
    else:
        out_shape = (jax.ShapeDtypeStruct(acc, F32), record)
        operands = (base, *xs, expert_in)
        in_specs = [SMEM] + [VMEM] * n_parts + [HBM]
    scratch.append(pltpu.SemaphoreType.DMA((RING, units // LANES)))
    return pl.pallas_call(
        functools.partial(expert_kernel, part, n_parts, reqs),
        out_shape=out_shape,
        in_specs=in_specs,
        out_specs=(VMEM,) * len(out_shape),
        scratch_shapes=scratch,
        compiler_params=pltpu.CompilerParams(vmem_limit_bytes=(23 if last else 19) * 2**20),
        cost_estimate=pl.CostEstimate(flops=10**9, bytes_accessed=100 * 10**6, transcendentals=0),
    )(*operands)


def local(
    n_pool, n_grp, n_shard,
    queries, new_kv, suffix_kv, suffix_len, prefix_pool, prefix_table, residual, norm_gain,
    expert_ids, gate_weights, expert_in, expert_down,
):
    reqs, width = queries.shape
    n_high = n_grp // 2
    flips = n_shard & (n_shard - 1) == 0

    def turn(a, d):
        pairs = [(i, i ^ abs(d) if flips else (i + d) % n_shard) for i in range(n_shard)]
        return lax.ppermute(a, "shard", pairs)

    def across(a, dp, dg):
        pairs = []
        for p in range(n_pool):
            for g in range(n_grp):
                to = (g // 2 + dg) % n_high * 2 + g % 2
                pairs.append((p * n_grp + g, (p + dp) % n_pool * n_grp + to))
        return lax.ppermute(a, ("pool", "grp"), pairs)

    def twin(a):
        return lax.ppermute(a, "grp", [(g, g ^ 1) for g in range(n_grp)])

    offsets = [(dp, dg) for dp in range(n_pool) for dg in range(n_high)][1:]
    base = (lax.axis_index("grp") * expert_in.shape[0]).astype(jnp.int32).reshape(1)

    def in_vmem(array):
        return pltpu.with_memory_space_constraint(array, pltpu.VMEM)

    def in_hbm(*arrays):
        return tuple(pltpu.with_memory_space_constraint(a, pltpu.HBM) for a in arrays)

    attended, sent = attend(
        *in_hbm(
            prefix_table, suffix_len, expert_ids.T, gate_weights.T, queries, new_kv, suffix_kv,
            prefix_pool, residual, norm_gain,
        )
    )
    (expert_in,) = in_hbm(expert_in)
    column = [sent] + [turn(sent, d) for d in range(1, n_shard)]
    cut = run_of(0, width)[1] + LANES
    columns = [jnp.concatenate(c, axis=0) for c in ([a[:, :cut] for a in column], [a[:, cut:] for a in column])]
    def aside(a):
        return [a] + [across(a, dp, dg) for dp, dg in offsets]

    rows_0 = aside(columns[0])
    rows_0 += [twin(a) for a in rows_0]
    acc, record = experts_of(0, reqs, base, rows_0, (), expert_in)
    rows_1 = aside(columns[1])
    acc, *rows_1 = lax.optimization_barrier((acc, *rows_1))
    rows_1 += [twin(a) for a in rows_1]
    near, far = experts_of(1, reqs, base, rows_1, (acc, record, in_vmem(expert_down)), expert_in)
    pair = (near.astype(F32) + twin(far).astype(F32)).astype(BF16)

    def home_along(a, total):
        a = a.reshape(n_shard, -1, a.shape[1])
        total = total + a[0].astype(F32)
        for d in range(1, n_shard):
            total += turn(a[d], -d).astype(F32)
        return total

    def home_aside(a, total):
        a = a.reshape(1 + len(offsets), -1, a.shape[1])
        total = total + a[0].astype(F32)
        for i, (dp, dg) in enumerate(offsets):
            total += across(a[i + 1], -dp, -dg).astype(F32)
        return total

    stream = (residual.astype(F32) + attended.astype(F32)).astype(BF16).astype(F32)
    out = home_along(home_aside(pair, 0.0).astype(BF16), stream)
    return attended, out.astype(BF16)


def solution(mesh):
    rows = P(ALL, None)
    in_specs = (
        rows,
        P(ALL, None, None),
        P(ALL, None, None, None),
        P(ALL),
        P(ALL, None, None, None, None),
        rows,
        rows,
        P(),
        rows,
        rows,
        P("grp", None, None, ("pool", "shard")),
        P("grp", ("pool", "shard"), None),
    )
    sizes = [mesh.shape[a] for a in ALL]
    return jax.shard_map(
        functools.partial(local, *sizes),
        mesh=mesh, in_specs=in_specs, out_specs=(rows, rows), check_vma=False,
    )
```
